32 devices in a mesh: seq: 8 (over y, x, core), tp: 4 (over z).
Axes of the slice: x: 2, y: 2, z: 4, core: 2. Of those that a mesh axis runs over, the one named last changes fastest.
Arguments:
- hidden_in: bfloat16 [8, 1024, 2048], P(None, 'seq', 'tp'), may hold values from -6 to 6
- cotangent: bfloat16 [8, 1024, 2048], P(None, 'seq', 'tp'), may hold values from -6 to 6
- valid_counts: int32 [8], replicated, may hold values from 51 to 1024, as said below
- pre_gain: float32 [2048], P('tp'), may hold values from 0.25 to 1.75
- pre_bias: float32 [2048], P('tp'), may hold values from -3 to 3
- qkv_weight: bfloat16 [2048, 3, 2048], P(None, None, 'tp'), may hold values from -0.125 to 0.125
- sub_gain: float32 [2048], P('tp'), may hold values from 0.25 to 1.75
- sub_bias: float32 [2048], P('tp'), may hold values from -3 to 3
- out_weight: bfloat16 [2048, 2048], P('tp'), may hold values from -0.125 to 0.125
- ffn_gain: float32 [2048], P('tp'), may hold values from 0.25 to 1.75
- ffn_bias: float32 [2048], P('tp'), may hold values from -3 to 3
- up_weight: bfloat16 [2048, 8192], P(None, 'tp'), may hold values from -0.125 to 0.125
- mid_gain: float32 [8192], P('tp'), may hold values from 0.25 to 1.75
- mid_bias: float32 [8192], P('tp'), may hold values from -3 to 3
- down_weight: bfloat16 [8192, 2048], P('tp'), may hold values from -0.0625 to 0.0625
Outputs:
- hidden_out: bfloat16 [8, 1024, 2048], P(None, 'seq', 'tp')
- input_grad: float32 [8, 1024, 2048], P(None, 'seq', 'tp')
- pregain_grad: float32 [2048], P('tp')
- prebias_grad: float32 [2048], P('tp')
- qkv_grad: float32 [2048, 3, 2048], P(None, None, 'tp')
- subgain_grad: float32 [2048], P('tp')
- subbias_grad: float32 [2048], P('tp')
- out_grad: float32 [2048, 2048], P('tp')
- ffngain_grad: float32 [2048], P('tp')
- ffnbias_grad: float32 [2048], P('tp')
- up_grad: float32 [2048, 8192], P(None, 'tp')
- midgain_grad: float32 [8192], P('tp')
- midbias_grad: float32 [8192], P('tp')
- down_grad: float32 [8192, 2048], P('tp')
The draws below stay inside these ranges and needn't reach their ends.
Inputs may be any that keep to these rules, and one draw needn't show every extreme that they name: `valid_counts`: the valid positions of a sequence come first; in every draw one sequence has all 1024 positions valid.
All inputs are finite; a program needn't handle non-finite values.
Results may differ from the reference program's by a relative error of at most 0.013.
The reference program's roundings to bfloat16 on the way count: a program that leaves them out, or rounds other values in their place, can miss the bound.
Values may be sent and summed in bfloat16 or wider, within the bound.
A program may use at most 320 MiB of HBM per device.

```python
import math
import jax
import jax.numpy as jnp
from jax import lax

D = 2048
HEADS = 32
FF = 8192
HD = 64
SEQS = 8
LEN = 1024


def draw_valid_counts(key, part):
    key = jax.random.fold_in(key, 11)
    first_key, second_key, third_key, full_key = jax.random.split(key, 4)
    shortest = max(1, LEN // 20)
    span = LEN - shortest + 1
    first = jax.random.randint(first_key, (SEQS,), 0, span)
    second = jax.random.randint(second_key, (SEQS,), 0, span)
    third = jax.random.randint(third_key, (SEQS,), 0, span)
    lengths = shortest + jnp.minimum(jnp.minimum(first, second), third)
    chosen = jax.random.randint(full_key, (), 0, SEQS)
    lengths = jnp.where(jnp.arange(SEQS) == chosen, LEN, lengths)
    return lengths.astype(jnp.int32)


def block_levels(rng, shape, cuts, least, top_value):
    def one(axis_at, parts):
        heights = jax.random.uniform(jax.random.fold_in(jax.random.fold_in(rng, 6), axis_at), (parts,), jnp.float32, least / len(cuts), top_value / len(cuts))
        return jnp.repeat(jnp.exp(heights), shape[axis_at] // parts).reshape((-1,) + (1,) * (len(shape) - axis_at - 1))

    loudness = one(*cuts[0])
    for cut in cuts[1:]:
        loudness = loudness * one(*cut)
    return loudness


def noise(stream_key, shape, deviation, most, pieces=(), kind=jnp.bfloat16):
    array = jax.random.normal(stream_key, shape, jnp.float32) * deviation
    if len(pieces) > 0:
        array = block_levels(stream_key, shape, pieces, -0.22, 0.18) * array
    return jnp.clip(array, min=-most, max=most).astype(kind)


def setup_inputs(seed: int = 0) -> dict:
    key_of = jax.random.split(jax.random.key(seed), 16)
    return {
        "hidden_in": noise(key_of[0], (SEQS, LEN, D), 1.0, 6.0, ((1, 8), (2, 4))),
        "cotangent": noise(key_of[1], (SEQS, LEN, D), 1.0, 6.0, ((1, 8), (2, 4))),
        "valid_counts": draw_valid_counts(jax.random.fold_in(key_of[15], 71), 0),
        "pre_gain": jnp.clip(1.0 + 0.15 * jax.random.normal(key_of[3], (D,), jnp.float32), 0.25, 1.75),
        "pre_bias": noise(key_of[4], (D,), 0.5, 3.0, ((0, 4),), jnp.float32),
        "qkv_weight": noise(key_of[5], (D, 3, HEADS * HD), D ** -0.5, 0.125, ((2, 4),)),
        "sub_gain": jnp.clip(1.0 + 0.15 * jax.random.normal(key_of[6], (HEADS * HD,), jnp.float32), 0.25, 1.75),
        "sub_bias": noise(key_of[7], (HEADS * HD,), 0.5, 3.0, ((0, 4),), jnp.float32),
        "out_weight": noise(key_of[8], (HEADS * HD, D), (HEADS * HD) ** -0.5, 0.125, ((0, 4),)),
        "ffn_gain": jnp.clip(1.0 + 0.15 * jax.random.normal(key_of[9], (D,), jnp.float32), 0.25, 1.75),
        "ffn_bias": noise(key_of[10], (D,), 0.5, 3.0, ((0, 4),), jnp.float32),
        "up_weight": noise(key_of[11], (D, FF), D ** -0.5, 0.125, ((1, 4),)),
        "mid_gain": jnp.clip(1.0 + 0.15 * jax.random.normal(key_of[12], (FF,), jnp.float32), 0.25, 1.75),
        "mid_bias": noise(key_of[13], (FF,), 0.5, 3.0, ((0, 4),), jnp.float32),
        "down_weight": noise(key_of[14], (FF, D), FF ** -0.5, 0.0625, ((0, 4),)),
    }


epsilon = 1e-05
masked_score = -1e+30
scale_base = 512.0
highest = lax.Precision.HIGHEST

@jax.custom_vjp
def low(v):
    return lax.optimization_barrier(v.astype(jnp.bfloat16)).astype(jnp.float32)

@jax.custom_vjp
def low_back(v):
    return v

def low_keep(v):
    return (low(v), None)

def low_pass(kept, grad):
    return (grad,)

def back_keep(v):
    return (v, None)

def back_low(kept, grad):
    return (low(grad),)
low.defvjp(low_keep, low_pass)
low_back.defvjp(back_keep, back_low)

def rotate_half(values, head_size):
    half = head_size // 2
    feature = jnp.arange(values.shape[-1]) % head_size
    return jnp.where(feature < half, -jnp.roll(values, -half, axis=-1), jnp.roll(values, half, axis=-1))

def xpos_tables(positions, width, head_size, length, sign):
    feature = jnp.arange(width) % head_size % (head_size // 2)
    index = feature.astype(jnp.float32)
    place = positions.astype(jnp.float32)
    inverse = jnp.power(10000.0, -2.0 * index / head_size)
    angle = place[:, None] * inverse[None, :]
    ratio = (2.0 * index + 0.4 * head_size) / (1.4 * head_size)
    shifted = (place - length // 2) / scale_base
    factor = jnp.exp(sign * jnp.log(ratio)[None, :] * shifted[:, None])
    return (jnp.cos(angle) * factor, jnp.sin(angle) * factor)

def rotate(values, cosine, sine):
    return values * cosine + rotate_half(values, HD) * sine

def norm(values, gain, bias):
    average = lax.optimization_barrier(jnp.mean(values, axis=-1, keepdims=True))
    spread = lax.rsqrt(lax.optimization_barrier(jnp.mean(values * values, axis=-1, keepdims=True)) - average * average + epsilon)
    return (values - average) * spread * gain + bias

def matmul(left, right):
    rows = left.reshape(-1, left.shape[-1])
    return jnp.dot(rows, right, precision=highest).reshape(left.shape[:-1] + (right.shape[-1],))

def head_attention(items):
    queries, keys, values, count = items
    place = jnp.arange(queries.shape[0])
    scores = low_back(jnp.dot(queries, keys.T, precision=highest) * HD ** (-0.5))
    allowed = (place[None, :] <= place[:, None]) & (place[None, :] < count)
    weights = low(jax.nn.softmax(jnp.where(allowed, scores, masked_score), axis=-1))
    return jnp.dot(weights, values, precision=highest)

def split_heads(values, group):
    return values.reshape(group, LEN, HEADS, HD).transpose(0, 2, 1, 3).reshape(group * HEADS, LEN, HD)

def merge_heads(values, group):
    return values.reshape(group, HEADS, LEN, HD).transpose(0, 2, 1, 3).reshape(group, LEN, HEADS * HD)

def layer(inputs, params, counts):
    pre_gain, pre_bias, qkv_weight, sub_gain, sub_bias, out_weight, ffn_gain, ffn_bias, up_weight, mid_gain, mid_bias, down_weight = params
    group = inputs.shape[0]
    attn_width = HEADS * HD
    place = jnp.arange(LEN)
    pre_rows = low(norm(inputs, pre_gain, pre_bias))
    projected = matmul(pre_rows, qkv_weight.reshape(D, 3 * attn_width)).reshape(group, LEN, 3, attn_width)
    query_cos, query_sin = xpos_tables(place, attn_width, HD, LEN, 1.0)
    key_cos, key_sin = xpos_tables(place, attn_width, HD, LEN, -1.0)
    queries = low(rotate(low_back(projected[:, :, 0]), query_cos, query_sin))
    keys = low(rotate(low_back(projected[:, :, 1]), key_cos, key_sin))
    values = low(low_back(projected[:, :, 2]))
    repeated = jnp.repeat(counts, HEADS)
    attended = lax.map(jax.checkpoint(head_attention), (split_heads(queries, group), split_heads(keys, group), split_heads(values, group), repeated))
    attended = low_back(merge_heads(attended, group))
    sub_rows = low(norm(attended, sub_gain, sub_bias))
    middle = inputs + low_back(matmul(sub_rows, out_weight))
    ffn_rows = low(norm(middle, ffn_gain, ffn_bias))
    raised = low_back(matmul(ffn_rows, up_weight))
    mid_rows = low(norm(jax.nn.gelu(raised, approximate=False), mid_gain, mid_bias))
    return middle + low_back(matmul(mid_rows, down_weight))

def reference(hidden_in, cotangent, valid_counts, pre_gain, pre_bias, qkv_weight, sub_gain, sub_bias, out_weight, ffn_gain, ffn_bias, up_weight, mid_gain, mid_bias, down_weight):
    params = tuple((weight.astype(jnp.float32) for weight in (pre_gain, pre_bias, qkv_weight, sub_gain, sub_bias, out_weight, ffn_gain, ffn_bias, up_weight, mid_gain, mid_bias, down_weight)))
    group = math.gcd(SEQS, max(1, 4096 // LEN))
    blocks = SEQS // group
    inputs = hidden_in.astype(jnp.float32).reshape(blocks, group, LEN, D)
    upstream = cotangent.astype(jnp.float32).reshape(blocks, group, LEN, D)
    counts = valid_counts.reshape(blocks, group)

    def one_group(totals, items):
        block_in, block_up, block_counts = items
        valid_mask = (jnp.arange(LEN)[None, :] < block_counts[:, None]).astype(jnp.float32)

        def forward(values, weights):
            return layer(values, weights, block_counts)
        result, pull = jax.vjp(forward, block_in, params)
        block_grad, weight_grads = pull(block_up * valid_mask[..., None])
        totals = jax.tree.map(jnp.add, totals, weight_grads)
        return (totals, (result.astype(jnp.bfloat16), block_grad))
    zeros = jax.tree.map(jnp.zeros_like, params)
    totals, (outputs, input_grads) = lax.scan(one_group, zeros, (inputs, upstream, counts))
    pregain_grad, prebias_grad, qkv_grad, subgain_grad, subbias_grad, out_grad, ffngain_grad, ffnbias_grad, up_grad, midgain_grad, midbias_grad, down_grad = totals
    return (outputs.reshape(SEQS, LEN, D), input_grads.reshape(SEQS, LEN, D), pregain_grad, prebias_grad, qkv_grad, subgain_grad, subbias_grad, out_grad, ffngain_grad, ffnbias_grad, up_grad, midgain_grad, midbias_grad, down_grad)
```

```python
import functools

import jax
import jax.numpy as jnp
from jax import lax
from jax.experimental import pallas as pl
from jax.experimental.pallas import tpu as pltpu
from jax.sharding import PartitionSpec as P

HD = 64
ROWS = 16
PAIR = 128
BUCKETS = (24, 28, 32, 40)

epsilon = 1e-05
masked_score = -1e30
scale_base = 512.0


def dot(left, right, dims, kind=jnp.float32):
    return lax.dot_general(left, right, (dims, ((), ())), preferred_element_type=kind)


def flat_product(left, right):
    return dot(left, right, ((1,), (0,)))


def weight_product(left, right):
    return dot(left, right, ((0,), (0,)))


def back_product(left, right):
    return dot(left, right, ((1,), (1,)))


def low(values):
    return values.astype(jnp.bfloat16)


def place_of(unit, row, shard, local_length, wide):
    piece = local_length // wide
    rounds = ROWS // piece
    if rounds == 1:
        return local_length * unit + piece * shard + row
    return local_length * (unit * rounds + row // piece) + piece * shard + row % piece


def masks(rows, keys, first_unit, valid_rows, count, shard, local_length, wide):
    row = lax.broadcasted_iota(jnp.int32, (rows, 1), 0)
    query_at = place_of(first_unit + row // ROWS, row % ROWS, shard, local_length, wide)
    key = lax.broadcasted_iota(jnp.int32, (1, keys), 1)
    span = ROWS * wide
    inner = key % span
    key_at = place_of(key // span, inner % ROWS, inner // ROWS, local_length, wide)
    allowed = (key_at <= query_at) & (key_at < count)
    return allowed & (row < valid_rows)


def stack_heads(rows):
    lane = lax.broadcasted_iota(jnp.int32, (1, PAIR), 1)
    zero = jnp.zeros_like(rows)
    return jnp.concatenate([jnp.where(lane < HD, rows, zero), jnp.where(lane >= HD, rows, zero)], axis=0)


def unstack_heads(rows):
    half = rows.shape[0] // 2
    lane = lax.broadcasted_iota(jnp.int32, (1, PAIR), 1)
    return jnp.where(lane < HD, rows[:half], rows[half:])


def forward_kernel(cases, length, local_length, wide, n_rows, n_keys, width, meta, q_hbm, kv_hbm, o_hbm, q, kv, o, sems):
    shard = lax.axis_index("seq")
    load_q = pltpu.make_async_copy(q_hbm, q.at[pl.ds(0, n_rows)], sems.at[0])
    load_kv = pltpu.make_async_copy(kv_hbm, kv.at[pl.ds(0, n_keys)], sems.at[1])
    load_q.start()
    load_kv.start()
    q[pl.ds(n_rows, q.shape[0] - n_rows), :] = jnp.zeros((q.shape[0] - n_rows, width), q.dtype)
    kv[pl.ds(n_keys, kv.shape[0] - n_keys), :] = jnp.zeros((kv.shape[0] - n_keys, 2 * width), kv.dtype)
    load_q.wait()
    load_kv.wait()
    span = ROWS * wide

    def one(b, carry):
        q_start = pl.multiple_of(meta[0, b] * ROWS, ROWS)
        first_unit = meta[1, b]
        units = meta[2, b]
        k_start = pl.multiple_of(meta[3, b] * span, span)
        count = meta[4, b]
        case = meta[5, b]
        valid_rows = meta[6, b] * ROWS

        for index, (rows, key_units) in enumerate(cases):
            keys = key_units * span

            @pl.when((case == index) & (valid_rows > 0))
            def _():
                allowed = masks(rows, keys, first_unit, valid_rows, count, shard, local_length, wide)
                bias = jnp.where(allowed, 0.0, masked_score).astype(jnp.float32)
                bias = jnp.concatenate([bias, bias], axis=0)
                for pair in range(width // PAIR):
                    at = pair * PAIR
                    stacked = stack_heads(q[pl.ds(q_start, rows), at : at + PAIR])
                    key_rows = kv[pl.ds(k_start, keys), at : at + PAIR]
                    value_rows = kv[pl.ds(k_start, keys), width + at : width + at + PAIR]
                    scores = dot(stacked, key_rows, ((1,), (1,))) * HD ** (-0.5) + bias
                    largest = jnp.max(scores, axis=1, keepdims=True)
                    raised = jnp.exp(scores - largest)
                    total = jnp.sum(raised, axis=1, keepdims=True)
                    mixed = dot(raised.astype(jnp.bfloat16), value_rows, ((1,), (0,))) / total
                    o[pl.ds(q_start, rows), at : at + PAIR] = unstack_heads(mixed)

        return carry

    lax.fori_loop(0, meta.shape[1], one, 0)
    store = pltpu.make_async_copy(o.at[pl.ds(0, n_rows)], o_hbm, sems.at[0])
    store.start()
    store.wait()


def backward_kernel(cases, length, local_length, wide, n_rows, n_keys, width, meta, q_hbm, kv_hbm, d_hbm, dq_hbm, dkv_hbm, q, kv, d, dq, dkv, sems):
    shard = lax.axis_index("seq")
    load_q = pltpu.make_async_copy(q_hbm, q.at[pl.ds(0, n_rows)], sems.at[0])
    load_kv = pltpu.make_async_copy(kv_hbm, kv.at[pl.ds(0, n_keys)], sems.at[1])
    load_d = pltpu.make_async_copy(d_hbm, d.at[pl.ds(0, n_rows)], sems.at[2])
    load_q.start()
    load_kv.start()
    load_d.start()
    q[pl.ds(n_rows, q.shape[0] - n_rows), :] = jnp.zeros((q.shape[0] - n_rows, width), q.dtype)
    d[pl.ds(n_rows, d.shape[0] - n_rows), :] = jnp.zeros((d.shape[0] - n_rows, width), d.dtype)
    kv[pl.ds(n_keys, kv.shape[0] - n_keys), :] = jnp.zeros((kv.shape[0] - n_keys, 2 * width), kv.dtype)
    load_q.wait()
    load_kv.wait()
    load_d.wait()
    span = ROWS * wide

    def one(b, carry):
        q_start = pl.multiple_of(meta[0, b] * ROWS, ROWS)
        first_unit = meta[1, b]
        k_start = pl.multiple_of(meta[3, b] * span, span)
        count = meta[4, b]
        case = meta[5, b]
        valid_rows = meta[6, b] * ROWS

        for index, (rows, key_units) in enumerate(cases):
            keys = key_units * span

            @pl.when(case == index)
            def _():
                allowed = masks(rows, keys, first_unit, valid_rows, count, shard, local_length, wide)
                bias = jnp.where(allowed, 0.0, masked_score).astype(jnp.float32)
                bias = jnp.concatenate([bias, bias], axis=0)
                for pair in range(width // PAIR):
                    at = pair * PAIR
                    stacked = stack_heads(q[pl.ds(q_start, rows), at : at + PAIR])
                    grads = stack_heads(d[pl.ds(q_start, rows), at : at + PAIR])
                    key_rows = kv[pl.ds(k_start, keys), at : at + PAIR]
                    value_rows = kv[pl.ds(k_start, keys), width + at : width + at + PAIR]
                    scores = dot(stacked, key_rows, ((1,), (1,))) * HD ** (-0.5) + bias
                    largest = jnp.maximum(jnp.max(scores, axis=1, keepdims=True), 0.1 * masked_score)
                    raised = jnp.exp(scores - largest)
                    total = jnp.sum(raised, axis=1, keepdims=True)
                    probs = raised * jnp.where(total > 0, 1.0 / jnp.where(total > 0, total, 1.0), 0.0)
                    prob_grad = dot(grads, value_rows, ((1,), (1,)))
                    offset = jnp.sum(probs * prob_grad, axis=1, keepdims=True)
                    score_grad = (probs * (prob_grad - offset)).astype(jnp.bfloat16)
                    dq[pl.ds(q_start, rows), at : at + PAIR] = unstack_heads(
                        dot(score_grad, key_rows, ((1,), (0,))) * HD ** (-0.5)
                    )
                    dkv[pl.ds(k_start, keys), at : at + PAIR] = (
                        dot(score_grad, stacked, ((0,), (0,))) * HD ** (-0.5)
                    ).astype(jnp.bfloat16)
                    dkv[pl.ds(k_start, keys), width + at : width + at + PAIR] = dot(
                        probs.astype(jnp.bfloat16), grads, ((0,), (0,))
                    ).astype(jnp.bfloat16)

        return carry

    lax.fori_loop(0, meta.shape[1], one, 0)
    store_q = pltpu.make_async_copy(dq.at[pl.ds(0, n_rows)], dq_hbm, sems.at[0])
    store_kv = pltpu.make_async_copy(dkv.at[pl.ds(0, n_keys)], dkv_hbm, sems.at[1])
    store_q.start()
    store_kv.start()
    store_q.wait()
    store_kv.wait()


def attention_params():
    return pltpu.CompilerParams(vmem_limit_bytes=60 * 1024 * 1024)


def attend_forward(meta, query_rows, kv_rows, cases, length, local_length, wide):
    n_rows, width = query_rows.shape
    n_keys = kv_rows.shape[0]
    pad_rows = max(rows for rows, _ in cases)
    pad_keys = max(units for _, units in cases) * ROWS * wide
    hbm = pl.BlockSpec(memory_space=pl.ANY)
    return pl.pallas_call(
        functools.partial(forward_kernel, cases, length, local_length, wide, n_rows, n_keys, width),
        out_shape=jax.ShapeDtypeStruct((n_rows, width), jnp.float32),
        grid_spec=pltpu.PrefetchScalarGridSpec(
            num_scalar_prefetch=1,
            grid=(1,),
            in_specs=[hbm, hbm],
            out_specs=hbm,
            scratch_shapes=[
                pltpu.VMEM((n_rows + pad_rows, width), jnp.bfloat16),
                pltpu.VMEM((n_keys + pad_keys, 2 * width), jnp.bfloat16),
                pltpu.VMEM((n_rows + pad_rows, width), jnp.float32),
                pltpu.SemaphoreType.DMA((2,)),
            ],
        ),
        compiler_params=attention_params(),
    )(meta, query_rows, kv_rows)


def attend_backward(meta, query_rows, kv_rows, grad_rows, cases, length, local_length, wide):
    n_rows, width = query_rows.shape
    n_keys = kv_rows.shape[0]
    pad_rows = max(rows for rows, _ in cases)
    pad_keys = max(units for _, units in cases) * ROWS * wide
    hbm = pl.BlockSpec(memory_space=pl.ANY)
    return pl.pallas_call(
        functools.partial(backward_kernel, cases, length, local_length, wide, n_rows, n_keys, width),
        out_shape=(
            jax.ShapeDtypeStruct((n_rows, width), jnp.float32),
            jax.ShapeDtypeStruct((n_keys, 2 * width), jnp.bfloat16),
        ),
        grid_spec=pltpu.PrefetchScalarGridSpec(
            num_scalar_prefetch=1,
            grid=(1,),
            in_specs=[hbm, hbm, hbm],
            out_specs=(hbm, hbm),
            scratch_shapes=[
                pltpu.VMEM((n_rows + pad_rows, width), jnp.bfloat16),
                pltpu.VMEM((n_keys + pad_keys, 2 * width), jnp.bfloat16),
                pltpu.VMEM((n_rows + pad_rows, width), jnp.bfloat16),
                pltpu.VMEM((n_rows + pad_rows, width), jnp.float32),
                pltpu.VMEM((n_keys + pad_keys, 2 * width), jnp.bfloat16),
                pltpu.SemaphoreType.DMA((3,)),
            ],
        ),
        compiler_params=attention_params(),
    )(meta, query_rows, kv_rows, grad_rows)


def flat_place(units, first_unit, local_length, wide, axis):
    each = units * ROWS
    shape = (wide * each, 1) if axis == 0 else (1, wide * each)
    at = lax.broadcasted_iota(jnp.int32, shape, axis)
    source = jnp.zeros_like(at)
    for k in range(1, wide):
        source += (at >= k * each).astype(jnp.int32)
    inner = at - source * each
    return inner // ROWS, place_of(first_unit + inner // ROWS, inner % ROWS, source, local_length, wide)


def swap(values):
    return pltpu.roll(values, HD, 1)


def low_lanes(values):
    lane = lax.broadcasted_iota(jnp.int32, (1, PAIR), 1)
    return jnp.where(lane < HD, values, jnp.zeros_like(values))


def join_lanes(left, right):
    lane = lax.broadcasted_iota(jnp.int32, (1, PAIR), 1)
    return jnp.where(lane < HD, left, swap(right))


def spread_halves(source, base, count, target):
    for k in range(source.shape[0]):
        pair = source[k, base : base + count // 2].astype(jnp.float32)
        target[k, 0 : count // 2] = low_lanes(pair).astype(target.dtype)
        target[k, count // 2 : count] = low_lanes(swap(pair)).astype(target.dtype)
        target[k, count:] = jnp.zeros((target.shape[1] - count, PAIR), target.dtype)


def fold_halves(source, count, target, base):
    for k in range(source.shape[0]):
        target[k, base : base + count // 2] = join_lanes(
            source[k, 0 : count // 2].astype(jnp.float32), source[k, count // 2 : count].astype(jnp.float32)
        ).astype(target.dtype)


def spread_keys(packed, n, queries, keys, values):
    for k in range(packed.shape[0]):
        both = packed[k, 0:n].astype(jnp.float32)
        if queries is not None:
            queries[k, 0:n] = low_lanes(both).astype(jnp.bfloat16)
            queries[k, n:] = jnp.zeros((queries.shape[1] - n, PAIR), jnp.bfloat16)
        keys[k, 0:n] = low_lanes(swap(both)).astype(jnp.bfloat16)
        keys[k, n:] = jnp.zeros((keys.shape[1] - n, PAIR), jnp.bfloat16)
    spread_halves(packed, n, n, values)


def rows_of(ref, start, count):
    return ref[:, pl.ds(start, count), :].reshape(ref.shape[0] * count, PAIR)


def head_forward_kernel(per, local_length, wide, n, meta, *refs):
    if len(refs) == 6:
        packed, out, queries, keys, values, mixed = refs
        spread_keys(packed, n, queries, keys, values)
        count_rows = n
    else:
        packed, others, out, queries, keys, values, mixed = refs
        spread_keys(packed, n, None, keys, values)
        count_rows = 2 * others.shape[1]
        spread_halves(others, 0, count_rows, queries)
    own = len(refs) == 6

    def one(b, carry):
        key_start = pl.multiple_of(meta[3, b] * ROWS, ROWS)
        count = meta[4, b]
        tiles = (meta[6, b] + 1) // 2

        def tile(t, carry):
            start = pl.multiple_of((meta[0, b] + 2 * t) * ROWS, ROWS)
            case = t if own else (meta[2, b] + 1) // 2 - 1
            for k in range(per // 2):
                units = 2 * (k + 1)

                @pl.when(case == k)
                def _():
                    _, query_at = flat_place(2, meta[1, b] + 2 * t, local_length, wide, 0)
                    _, key_at = flat_place(units, 0, local_length, wide, 1)
                    key_rows = rows_of(keys, key_start, units * ROWS)
                    value_rows = rows_of(values, key_start, units * ROWS)
                    scores = dot(rows_of(queries, start, 2 * ROWS), key_rows, ((1,), (1,))) * HD ** (-0.5)
                    limit = jnp.minimum(query_at, count - 1)
                    scores = jnp.where(key_at <= limit, scores, masked_score)
                    largest = jnp.max(scores, axis=1, keepdims=True)
                    raised = jnp.exp(scores - largest)
                    total = jnp.sum(raised, axis=1, keepdims=True)
                    result = dot(raised.astype(jnp.bfloat16), value_rows, ((1,), (0,))) / total
                    mixed[:, pl.ds(start, 2 * ROWS), :] = result.reshape(wide, 2 * ROWS, PAIR)

            return carry

        return lax.fori_loop(0, tiles, tile, carry)

    lax.fori_loop(0, meta.shape[1], one, 0)
    fold_halves(mixed, count_rows, out, 0)


def head_backward_kernel(per, local_length, wide, n, meta, packed, grads_in, out, queries, keys, values, grads, dq, dk, dv):
    spread_keys(packed, n, queries, keys, values)
    spread_halves(grads_in, 0, n, grads)
    dk[...] = jnp.zeros_like(dk)
    dv[...] = jnp.zeros_like(dv)

    def one(b, carry):
        key_start = pl.multiple_of(meta[3, b] * ROWS, ROWS)
        count = meta[4, b]
        tiles = (meta[6, b] + 1) // 2

        def tile(t, carry):
            start = pl.multiple_of((meta[0, b] + 2 * t) * ROWS, ROWS)
            for k in range(per // 2):
                units = 2 * (k + 1)

                @pl.when(t == k)
                def _():
                    query_unit, query_at = flat_place(2, 2 * k, local_length, wide, 0)
                    _, key_at = flat_place(units, 0, local_length, wide, 1)
                    query_rows = rows_of(queries, start, 2 * ROWS)
                    grad_rows = rows_of(grads, start, 2 * ROWS)
                    key_rows = rows_of(keys, key_start, units * ROWS)
                    value_rows = rows_of(values, key_start, units * ROWS)
                    scores = dot(query_rows, key_rows, ((1,), (1,))) * HD ** (-0.5)
                    limit = jnp.minimum(query_at, count - 1)
                    scores = jnp.where(key_at <= limit, scores, masked_score)
                    largest = jnp.max(scores, axis=1, keepdims=True)
                    raised = jnp.exp(scores - largest)
                    total = jnp.sum(raised, axis=1, keepdims=True)
                    there = query_unit + 2 * k < meta[6, b]
                    probs = raised * jnp.where(there, 1.0 / total, 0.0)
                    prob_grad = dot(grad_rows, value_rows, ((1,), (1,)))
                    offset = jnp.sum(probs * prob_grad, axis=1, keepdims=True)
                    score_grad = (probs * (prob_grad - offset)).astype(jnp.bfloat16)
                    shape = (wide, 2 * ROWS, PAIR)
                    dq[:, pl.ds(start, 2 * ROWS), :] = (dot(score_grad, key_rows, ((1,), (0,))) * HD ** (-0.5)).reshape(shape)
                    shape = (wide, units * ROWS, PAIR)
                    dk[:, pl.ds(key_start, units * ROWS), :] += (
                        dot(score_grad, query_rows, ((0,), (0,))) * HD ** (-0.5)
                    ).reshape(shape)
                    dv[:, pl.ds(key_start, units * ROWS), :] += dot(
                        probs.astype(jnp.bfloat16), grad_rows, ((0,), (0,))
                    ).reshape(shape)

            return carry

        return lax.fori_loop(0, tiles, tile, carry)

    lax.fori_loop(0, meta.shape[1], one, 0)
    for k in range(wide):
        out[k, 0:n] = join_lanes(dq[k, 0:n], dk[k, 0:n]).astype(jnp.bfloat16)
    fold_halves(dv, n, out, n)


def whole(shape):
    return pl.BlockSpec(shape, lambda i, meta: (0,) * len(shape))


def head_call(kernel, meta, arrays, out_shape, scratch, cost):
    flops, exps = cost
    return pl.pallas_call(
        kernel,
        out_shape=jax.ShapeDtypeStruct(out_shape, jnp.bfloat16),
        grid_spec=pltpu.PrefetchScalarGridSpec(
            num_scalar_prefetch=1,
            grid=(1,),
            in_specs=[whole(array.shape) for array in arrays],
            out_specs=whole(out_shape),
            scratch_shapes=[pltpu.VMEM(shape, kind) for shape, kind in scratch],
        ),
        compiler_params=attention_params(),
        cost_estimate=pl.CostEstimate(flops=flops, bytes_accessed=4 << 20, transcendentals=exps),
    )(meta, *arrays)


def head_forward(meta, packed, others, per, local_length):
    wide = packed.shape[0]
    n = packed.shape[1] * 2 // 3
    rows = n if others is None else 2 * others.shape[1]
    kept, mine = (wide, n + 2 * ROWS, PAIR), (wide, rows + 2 * ROWS, PAIR)
    scratch = [(mine, jnp.bfloat16), (kept, jnp.bfloat16), (kept, jnp.bfloat16), (mine, jnp.float32)]
    return head_call(
        functools.partial(head_forward_kernel, per, local_length, wide, n),
        meta,
        [packed] + ([] if others is None else [others]),
        (wide, rows // 2, PAIR),
        scratch,
        (4 << 30, 4 << 20),
    )


def head_backward(meta, packed, grads, per, local_length):
    wide = packed.shape[0]
    n = packed.shape[1] * 2 // 3
    kept = (wide, n + 2 * ROWS, PAIR)
    return head_call(
        functools.partial(head_backward_kernel, per, local_length, wide, n),
        meta,
        [packed, grads],
        packed.shape,
        [(kept, jnp.bfloat16)] * 4 + [(kept, jnp.float32)] * 3,
        (8 << 30, 4 << 20),
    )


def turn(values):
    lane = lax.broadcasted_iota(jnp.int32, (1, PAIR), 1)
    return jnp.where(lane % HD < HD // 2, -pltpu.roll(values, PAIR - HD // 2, 1), pltpu.roll(values, HD // 2, 1))


def split_pair(values, other, head):
    lane = lax.broadcasted_iota(jnp.int32, (1, PAIR), 1)
    if head == 0:
        return jnp.where(lane < HD, values, swap(other))
    return jnp.where(lane < HD, swap(values), other)


def chunk_of(half):
    return next(size for size in (64, 32, 16) if half % size == 0)


def pack_kernel(n, tables, *refs):
    out = refs[-1]
    half = n // 2
    step = chunk_of(half)
    pairs = out.shape[0] // 2

    def turned(ref, rows, at, cosine, sine):
        values = ref[rows, at : at + PAIR].astype(jnp.float32)
        if cosine is None:
            return values
        return values * cosine[rows, :] + turn(values) * sine[rows, :]

    def one(c, carry):
        top = pl.ds(pl.multiple_of(c * step, step), step)
        bottom = pl.ds(pl.multiple_of(half + c * step, ROWS), step)
        for pair in range(pairs):
            at = pair * PAIR
            if tables == 4:
                q, k, v, qc, qs, kc, ks = refs[:7]
                for rows in (top, bottom):
                    query, key = turned(q, rows, at, qc, qs), turned(k, rows, at, kc, ks)
                    for head in range(2):
                        out[2 * pair + head, rows, :] = split_pair(query, key, head).astype(jnp.bfloat16)
                single, base, cosine, sine = v, n, None, None
            else:
                single, base = refs[0], 0
                cosine, sine = (refs[1], refs[2]) if tables == 2 else (None, None)
            first, second = (turned(single, rows, at, cosine, sine) for rows in (top, bottom))
            rows = pl.ds(pl.multiple_of(base + c * step, ROWS), step)
            for head in range(2):
                out[2 * pair + head, rows, :] = split_pair(first, second, head).astype(jnp.bfloat16)
        return carry

    lax.fori_loop(0, half // step, one, 0)


def pack(arrays, tables):
    n, width = arrays[0].shape
    rows = n // 2 + (n if len(arrays) == 3 else 0)
    return pl.pallas_call(
        functools.partial(pack_kernel, n, len(tables)),
        out_shape=jax.ShapeDtypeStruct((width // HD, rows, PAIR), jnp.bfloat16),
        compiler_params=attention_params(),
    )(*arrays, *tables)


def unpack_kernel(n, tables, packed, *refs):
    out = refs[-1]
    half = n // 2
    step = chunk_of(half)
    width = packed.shape[0] * HD
    base = n if tables else 0

    def unturned(values, rows, cosine, sine):
        return cosine[rows, :] * values - turn(sine[rows, :] * values)

    def one(c, carry):
        top = pl.ds(pl.multiple_of(c * step, step), step)
        bottom = pl.ds(pl.multiple_of(half + c * step, ROWS), step)
        double = pl.ds(pl.multiple_of(base + c * step, ROWS), step)
        for pair in range(width // PAIR):
            at = pair * PAIR
            if tables:
                qc, qs, kc, ks = refs[:4]
                for rows in (top, bottom):
                    even = packed[2 * pair, rows, :].astype(jnp.float32)
                    odd = packed[2 * pair + 1, rows, :].astype(jnp.float32)
                    query, key = split_pair(even, odd, 0), split_pair(even, odd, 1)
                    out[rows, at : at + PAIR] = unturned(query, rows, qc, qs).astype(jnp.bfloat16)
                    out[rows, width + at : width + at + PAIR] = unturned(key, rows, kc, ks).astype(jnp.bfloat16)
            even = packed[2 * pair, double, :].astype(jnp.float32)
            odd = packed[2 * pair + 1, double, :].astype(jnp.float32)
            at = at + (2 * width if tables else 0)
            out[top, at : at + PAIR] = split_pair(even, odd, 0).astype(jnp.bfloat16)
            out[bottom, at : at + PAIR] = split_pair(even, odd, 1).astype(jnp.bfloat16)
        return carry

    lax.fori_loop(0, half // step, one, 0)


def unpack(packed, tables):
    heads, rows, _ = packed.shape
    n = rows * 2 // 3 if tables else rows * 2
    return pl.pallas_call(
        functools.partial(unpack_kernel, n, len(tables)),
        out_shape=jax.ShapeDtypeStruct((n, heads * HD * (3 if tables else 1)), jnp.bfloat16),
        compiler_params=attention_params(),
    )(packed, *tables)


def exchange(values):
    return lax.all_to_all(values, "seq", 0, 0, tiled=True)


def reorder_kernel(index, source, result):
    def one(i, carry):
        result[i] = source[index[i]]
        return carry

    lax.fori_loop(0, result.shape[0], one, 0)


def reorder(units, index):
    return pl.pallas_call(
        reorder_kernel,
        out_shape=jax.ShapeDtypeStruct(index.shape + units.shape[1:], units.dtype),
        grid_spec=pltpu.PrefetchScalarGridSpec(
            num_scalar_prefetch=1,
            grid=(1,),
            in_specs=[pl.BlockSpec(units.shape, lambda i, index: (0, 0, 0))],
            out_specs=pl.BlockSpec(index.shape + units.shape[1:], lambda i, index: (0, 0, 0)),
        ),
    )(index.astype(jnp.int32), units)


def xpos_tables(place, length, sign):
    feature = jnp.arange(PAIR) % (HD // 2)
    index = feature.astype(jnp.float32)
    place = place.astype(jnp.float32)
    inverse = jnp.power(10000.0, -2.0 * index / HD)
    angle = place[:, None] * inverse[None, :]
    ratio = (2.0 * index + 0.4 * HD) / (1.4 * HD)
    shifted = (place - length // 2) / scale_base
    factor = jnp.exp(sign * jnp.log(ratio)[None, :] * shifted[:, None])
    return jnp.cos(angle) * factor, jnp.sin(angle) * factor


def rotate_half(values):
    half = HD // 2
    feature = jnp.arange(values.shape[-1]) % HD
    return jnp.where(feature < half, -jnp.roll(values, -half, axis=-1), jnp.roll(values, half, axis=-1))


def widen(tables, width):
    return [jnp.concatenate([table] * (width // PAIR), axis=1) for table in tables]


def rotate(values, tables):
    cosine, sine = widen(tables, values.shape[1])
    return values * cosine + rotate_half(values) * sine


def unrotate(grads, tables):
    cosine, sine = widen(tables, grads.shape[1])
    return cosine * grads - rotate_half(sine * grads)


def row_stats(values, width):
    average = jnp.sum(values, axis=-1, keepdims=True) / width
    spread = lax.rsqrt(jnp.sum(values * values, axis=-1, keepdims=True) / width - average * average + epsilon)
    return average, spread


def gather_tp(values):
    return lax.all_gather(values, "tp", axis=1, tiled=True)


def scatter_tp(values):
    return lax.psum_scatter(values, "tp", scatter_dimension=1, tiled=True)


def total_tp(values):
    return gather_tp(scatter_tp(values))


def along_line(values, step, first, last):
    size = lax.axis_size("tp")
    pairs = [(i, i + step) for i in range(size) if first <= i <= last and 0 <= i + step < size]
    return lax.ppermute(values, "tp", pairs)


def gather_line(values):
    size, me, width = lax.axis_size("tp"), lax.axis_index("tp"), values.shape[1]
    up, down = [values], [values]
    for step in range(1, size):
        up.append(along_line(up[-1], 1, step - 1, size))
        down.append(along_line(down[-1], -1, 0, size - step))
    whole = jnp.zeros((values.shape[0], width * size), values.dtype)
    for step in range(size):
        piece = values if step == 0 else jnp.where(me >= step, up[step], down[size - step])
        whole = lax.dynamic_update_slice_in_dim(whole, piece, ((me - step) % size) * width, axis=1)
    return whole


def scatter_line(values):
    size, me = lax.axis_size("tp"), lax.axis_index("tp")
    width = values.shape[1] // size

    def part(step):
        return lax.dynamic_slice_in_dim(values, ((me + step) % size) * width, width, axis=1)

    up = down = None
    for step in range(1, size):
        right, left = part(size - step), part(step - size)
        up = along_line(right if up is None else right + up, 1, 0, step - 1)
        down = along_line(left if down is None else left + down, -1, size - step, size)
    return (part(0).astype(jnp.float32) + up.astype(jnp.float32) + down.astype(jnp.float32)).astype(values.dtype)


def total_line(values):
    return gather_line(scatter_line(values))


def small_total_tp(values):
    size = lax.axis_size("tp")
    result = values
    for step in range(1, size):
        result = result + lax.ppermute(values, "tp", [(i, (i + step) % size) for i in range(size)])
    return result


def partner(values, bit):
    size = lax.axis_size("seq")
    return lax.ppermute(values, "seq", [(i, i ^ (1 << bit)) for i in range(size)])


def small_total_seq(values):
    for bit in range(lax.axis_size("seq").bit_length() - 1):
        values = values + partner(values, bit)
    return values


def place_kernel(each, index, *refs):
    *sources, result = refs
    i = pl.program_id(0)
    for k, source in enumerate(sources):

        @pl.when(i // each == k)
        def _():
            columns = result.shape[2]
            for part in range(result.shape[0]):
                result[part] = source[0, :, part * columns : (part + 1) * columns].astype(jnp.float32)


def place_pieces(sources, index, parts):
    each, rows, columns = sources[0].shape
    total = each * len(sources)
    wide = columns // parts

    def source_at(k):
        return lambda i, index: (jnp.clip(i - k * each, 0, each - 1), 0, 0)

    return pl.pallas_call(
        functools.partial(place_kernel, each),
        out_shape=jax.ShapeDtypeStruct((parts, total * rows, wide), jnp.float32),
        grid_spec=pltpu.PrefetchScalarGridSpec(
            num_scalar_prefetch=1,
            grid=(total,),
            in_specs=[pl.BlockSpec((1, rows, columns), source_at(k)) for k in range(len(sources))],
            out_specs=pl.BlockSpec((parts, rows, wide), lambda i, index: (0, index[i], 0)),
        ),
        compiler_params=pltpu.CompilerParams(vmem_limit_bytes=40 * 1024 * 1024),
    )(index.astype(jnp.int32), *sources)


def place_two(first, second):
    sources, places = [], []
    for k, (arrays, index) in enumerate((first, second)):
        sources += arrays
        inner = index.shape[0] // 2
        places.append((index // inner * 2 + k) * inner + index % inner)
    return place_pieces(sources, jnp.concatenate(places), 3)


def core_half(left, right):
    me = lax.axis_index("seq") & 1
    size = left.shape[1] // 2

    def part(which):
        return weight_product(lax.dynamic_slice_in_dim(left, which * size, size, axis=1), right)

    got = partner(low(part(1 - me)), 0)
    return low(part(me) + got.astype(jnp.float32))


def total_cube(halves):
    bits = lax.axis_size("seq").bit_length() - 1
    me = lax.axis_index("seq")

    def own(bit):
        return (me >> bit) & 1

    def part(array, which):
        size = array.shape[0] // 2
        return lax.dynamic_slice_in_dim(array, which * size, size, axis=0)

    results = []
    for current, flipped in halves:
        order = list(range(1, bits))
        if flipped:
            order = order[::-1]
        for bit in order:
            current = part(current, own(bit)) + partner(part(current, 1 - own(bit)), bit)
        current = current[None]
        distance = [0]
        for bit in reversed(order):
            current = jnp.concatenate([current, partner(current, bit)], axis=0)
            distance = distance + [d ^ (1 << bit) for d in distance]
        sources, places = [], []
        for array, flip in ((current, 0), (partner(current, 0), 1)):
            sources.append(array)
            for d in distance:
                who = me ^ (d ^ flip)
                at = who & 1
                for bit in order:
                    at = at * 2 + ((who >> bit) & 1)
                places.append(at)
        results.append((sources, jnp.stack(places)))
    return results


def after(value, *others):
    return lax.optimization_barrier((value,) + others)[0]


def own_columns(values, width):
    return lax.dynamic_slice_in_dim(values, lax.axis_index("tp") * width, width, axis=1)


def partial_gelu(values):
    return jax.nn.gelu(values, approximate=False)


def body(v_units, hidden_in, cotangent, counts, vectors, weights):
    (pre_gain, pre_bias, sub_gain, sub_bias, ffn_gain, ffn_bias, mid_gain, mid_bias) = vectors
    qkv_weight, out_weight, up_weight, down_weight = weights
    wide = lax.axis_size("seq")
    tp = lax.axis_size("tp")
    shard = lax.axis_index("seq")
    sequences, local_length, local_width = hidden_in.shape
    n_units = sequences * local_length // ROWS
    per = n_units // sequences
    piece = local_length // wide
    length = local_length * wide
    span = ROWS * wide
    model_width = local_width * tp
    attn_local = out_weight.shape[0]
    attn_width = attn_local * tp
    hidden_local = up_weight.shape[1]
    hidden_width = hidden_local * tp
    nv = v_units * ROWS
    np_ = (n_units - v_units) * ROWS

    need = (counts + span - 1) // span
    room = per - need
    extra = v_units - jnp.sum(need)
    which = jnp.arange(sequences)
    before = jnp.sum(jnp.where(which[None, :] < which[:, None], room[None, :], 0), axis=1)
    taken = need + jnp.clip(extra - before, 0, room)
    offset = jnp.sum(jnp.where(which[None, :] < which[:, None], taken[None, :], 0), axis=1)
    unit = jnp.arange(n_units)
    unit_b, unit_u = unit // per, unit % per
    picked = unit_u[None, :] < taken[:, None]
    mine = unit_b[None, :] == which[:, None]
    taken_of = jnp.sum(jnp.where(mine, taken[:, None], 0), axis=0)
    offset_of = jnp.sum(jnp.where(mine, offset[:, None], 0), axis=0)
    rank = jnp.where(
        unit_u < taken_of,
        offset_of + unit_u,
        v_units + (unit_b * per - offset_of) + (unit_u - taken_of),
    )
    order = jnp.sum(jnp.where(rank[None, :] == unit[:, None], unit[None, :], 0), axis=1)
    count_of = jnp.sum(jnp.where(mine, counts[:, None], 0), axis=0)

    row = jnp.arange(ROWS)
    place = place_of((order % per)[:, None], row[None, :], shard, local_length, wide).reshape(-1)
    del picked

    cases_v = ((2 * ROWS, 2), (4 * ROWS, 4), (per * ROWS, per))
    cases_p = (((per - 1) * ROWS, 2), ((per - 3) * ROWS, 4), ((per - 5) * ROWS, per))
    case = jnp.where(taken <= 2, 0, jnp.where(taken <= 4, 1, 2))
    zero = jnp.zeros_like(offset)
    meta_v = jnp.stack([offset, zero, taken, offset, counts, case, taken]).astype(jnp.int32)
    meta_p = jnp.stack([which * per - offset, taken, taken, offset, counts, case, per - taken]).astype(jnp.int32)
    geometry = (length, local_length, wide)

    def stripe(values):
        pieces = values.reshape(sequences, wide, piece, local_width)
        pieces = lax.all_to_all(pieces, "seq", 1, 1, tiled=True)
        return pieces.reshape(n_units, ROWS, local_width)

    def unstripe(units):
        pieces = units.reshape(sequences, wide, piece, local_width)
        pieces = lax.all_to_all(pieces, "seq", 1, 1, tiled=True)
        return pieces.reshape(sequences, local_length, local_width)

    x_order = reorder(stripe(hidden_in), order)
    lines = jnp.stack([pre_gain, pre_bias, ffn_gain, ffn_bias])
    split = []
    for _ in range(3):
        split.append(lax.reduce_precision(lines, 8, 7))
        lines = lines - split[-1]
    split.append(jnp.zeros_like(lines))
    split = low(jnp.concatenate(split, axis=0))
    gathered = gather_tp(jnp.concatenate([x_order[:v_units].reshape(nv, local_width), split], axis=0))
    xv = gathered[:nv]
    lines = gathered[nv:].astype(jnp.float32)
    lines = lines[0:4] + lines[4:8] + lines[8:12]
    pre_gain_all, pre_bias_all, ffn_gain_all, ffn_bias_all = (lines[i : i + 1] for i in range(4))
    out_f32 = out_weight.astype(jnp.float32)
    out_lines = small_total_tp(
        jnp.stack([jnp.sum(sub_gain[:, None] * out_f32, axis=0), jnp.sum(sub_bias[:, None] * out_f32, axis=0)])
    )
    c_units = reorder(stripe(after(cotangent, x_order)), order[:v_units])
    count_at = jnp.sum(jnp.where(order[:, None] == unit[None, :], count_of[None, :], 0), axis=1)
    count_rows = jnp.broadcast_to(count_at[:v_units, None], (v_units, ROWS)).reshape(-1)
    valid = (place[:nv] < count_rows)[:, None]
    c_rows = jnp.where(valid, c_units.reshape(nv, local_width), 0).astype(jnp.bfloat16)

    place_v, place_p = place[:nv], place[nv:]
    query_tables = xpos_tables(place_v, length, 1.0)
    key_tables = xpos_tables(place_v, length, -1.0)
    qkv_parts = [qkv_weight[:, i] for i in range(3)]

    def pre(rows):
        values = rows.astype(jnp.float32)
        average, spread = row_stats(values, model_width)
        normed = (values - average) * spread
        return low(normed * pre_gain_all + pre_bias_all), average, spread

    one_head = attn_local == HD * wide
    pre_v, pre_average, pre_spread = pre(after(xv, c_units))
    raw = [flat_product(pre_v, part) for part in qkv_parts]
    if one_head:
        packed = exchange(pack(raw, query_tables + key_tables))
    else:
        own_kv = low(jnp.concatenate([rotate(raw[1], key_tables), raw[2]], axis=1))
        kv = lax.all_gather(own_kv.reshape(v_units, ROWS, 2 * attn_local), "seq", axis=1, tiled=True)
        kv = kv.reshape(v_units * span, 2 * attn_local)
        queries_v = low(rotate(raw[0], query_tables))
    others = gather_line(after(jnp.concatenate([c_rows, x_order[v_units:].reshape(np_, local_width)], axis=0), xv))
    cv, xp = others[:nv], others[nv:]

    def sub_norm(attended):
        sums = small_total_tp(jnp.stack([jnp.sum(attended, axis=1), jnp.sum(attended * attended, axis=1)]))
        average = (sums[0] / attn_width)[:, None]
        spread = lax.rsqrt((sums[1] / attn_width)[:, None] - average * average + epsilon)
        normed = (attended - average) * spread
        return normed, spread, low(normed * sub_gain + sub_bias)

    def ffn_norm(rows, branch):
        middle = rows.astype(jnp.float32) + branch.astype(jnp.float32)
        average, spread = row_stats(middle, model_width)
        normed = (middle - average) * spread
        return middle, normed, spread, low(normed * ffn_gain_all + ffn_bias_all)

    if one_head:
        attended = unpack(exchange(head_forward(meta_v, packed, None, per, local_length)), ())
    else:
        attended = attend_forward(meta_v, queries_v, kv, cases_v, *geometry)
    attended = after(attended, others).astype(jnp.float32)
    sub_normed, sub_spread, sub_rows = sub_norm(attended)
    branch = total_tp(low(flat_product(sub_rows, out_weight)))
    mid_grad = back_product(cv, down_weight)
    if np_:
        pre_p, _, _ = pre(xp)
        query_p = flat_product(pre_p, qkv_parts[0])
        tables_p = xpos_tables(place_p, length, 1.0)
        if one_head:
            attended_p = exchange(head_forward(meta_p, packed, exchange(pack([query_p], tables_p)), per, local_length))
            attended_p = unpack(attended_p, ())
        else:
            attended_p = attend_forward(meta_p, low(rotate(query_p, tables_p)), kv, cases_p, *geometry)
        _, _, sub_p = sub_norm(attended_p.astype(jnp.float32))
        branch_p = after(low(flat_product(sub_p, out_weight)), branch)
        branch, branch_p, mid_grad = lax.optimization_barrier((branch, branch_p, mid_grad))
        branch_p = total_tp(branch_p)

    middle, ffn_normed, ffn_spread, ffn_rows = ffn_norm(xv, branch)
    raised = flat_product(ffn_rows, up_weight)
    activated, gelu_pull = jax.vjp(partial_gelu, raised)
    scaled = mid_grad * mid_gain
    sums = small_total_tp(
        jnp.stack(
            [
                jnp.sum(activated, axis=1),
                jnp.sum(activated * activated, axis=1),
                jnp.sum(scaled, axis=1),
                jnp.sum(scaled * activated, axis=1),
            ]
        )
    )
    average = (sums[0] / hidden_width)[:, None]
    mid_spread = lax.rsqrt((sums[1] / hidden_width)[:, None] - average * average + epsilon)
    mid_normed = (activated - average) * mid_spread
    mid_rows = low(mid_normed * mid_gain + mid_bias)
    total = (sums[2] / hidden_width)[:, None]
    along = (sums[3] / hidden_width)[:, None]
    along = mid_spread * (along - average * total)
    act_grad = mid_spread * (scaled - total - mid_normed * along)
    raised_grad = low(gelu_pull(act_grad)[0])
    ffnin_part = low(back_product(raised_grad, up_weight))
    if np_:
        ffnin_part = after(ffnin_part, branch_p)
    ffnin = total_tp(ffnin_part)

    midgain_grad = jnp.sum(mid_grad * mid_normed, axis=0)
    midbias_grad = jnp.sum(mid_grad, axis=0)
    ffn_halves = core_half(mid_rows, cv), core_half(ffn_rows, raised_grad)
    down_part = low(flat_product(mid_rows, down_weight))
    if np_:
        middle_p, _, _, ffn_p = ffn_norm(xp, branch_p)
        activated_p = partial_gelu(flat_product(ffn_p, up_weight))
        sums = small_total_tp(jnp.stack([jnp.sum(activated_p, axis=1), jnp.sum(activated_p * activated_p, axis=1)]))
        average = (sums[0] / hidden_width)[:, None]
        spread = lax.rsqrt((sums[1] / hidden_width)[:, None] - average * average + epsilon)
        mid_p = low((activated_p - average) * spread * mid_gain + mid_bias)
        down_part = jnp.concatenate([down_part, low(flat_product(mid_p, down_weight))], axis=0)
        middle_own = jnp.concatenate([own_columns(middle, local_width), own_columns(middle_p, local_width)], axis=0)
    else:
        middle_own = own_columns(middle, local_width)

    ffnin, down_part, *ffn_halves = lax.optimization_barrier((ffnin, down_part) + ffn_halves)
    down_pieces, up_pieces = total_cube([(ffn_halves[0], False), (ffn_halves[1], True)])
    ffnin = ffnin.astype(jnp.float32)
    scaled = ffnin * ffn_gain_all
    total = jnp.sum(scaled, axis=1, keepdims=True) / model_width
    along = jnp.sum(scaled * ffn_normed, axis=1, keepdims=True) / model_width
    middle_grad = cv.astype(jnp.float32) + ffn_spread * (scaled - total - ffn_normed * along)
    branch_rows = low(middle_grad)
    ffngain_grad = jnp.sum(own_columns(ffnin * ffn_normed, local_width), axis=0)
    ffnbias_grad = jnp.sum(own_columns(ffnin, local_width), axis=0)
    out_half = core_half(sub_rows, branch_rows)

    sub_grad = back_product(branch_rows, out_weight)
    branch_f32 = branch_rows.astype(jnp.float32)
    total = jnp.sum(branch_f32 * out_lines[0:1], axis=1, keepdims=True) / attn_width
    along = jnp.sum(branch_f32 * (branch.astype(jnp.float32) - out_lines[1:2]), axis=1, keepdims=True) / attn_width
    attended_grad = low(sub_spread * (sub_grad * sub_gain - total - sub_normed * along))
    subgain_grad = jnp.sum(sub_grad * sub_normed, axis=0)
    subbias_grad = jnp.sum(sub_grad, axis=0)

    if one_head:
        grads = head_backward(meta_v, packed, exchange(pack([attended_grad], ())), per, local_length)
        projected_grad = unpack(exchange(grads), query_tables + key_tables)
    else:
        query_grad, kv_grad = attend_backward(meta_v, queries_v, kv, attended_grad, cases_v, *geometry)
        kv_grad = lax.psum_scatter(kv_grad.reshape(v_units, span, 2 * attn_local), "seq", scatter_dimension=1, tiled=True)
        kv_grad = kv_grad.reshape(nv, 2 * attn_local).astype(jnp.float32)
        projected_grad = [
            unrotate(query_grad, query_tables),
            unrotate(kv_grad[:, :attn_local], key_tables),
            kv_grad[:, attn_local:],
        ]
        projected_grad = low(jnp.concatenate(projected_grad, axis=1))
    out_all = low(middle_own + scatter_tp(after(down_part, branch_rows)).astype(jnp.float32))
    hidden_out = unstripe(reorder(out_all.reshape(n_units, ROWS, local_width), rank))

    prein = sum(
        back_product(projected_grad[:, i * attn_local : (i + 1) * attn_local], part) for i, part in enumerate(qkv_parts)
    )
    prein = scatter_tp(low(prein)).astype(jnp.float32)
    qkv_half = core_half(pre_v, projected_grad)
    size = qkv_half.shape[0] // 2
    out_pieces, first_pieces, second_pieces = total_cube(
        [(out_half, False), (qkv_half[:size], False), (qkv_half[size:], True)]
    )

    own_x = x_order[:v_units].reshape(nv, local_width).astype(jnp.float32)
    pre_normed = (own_x - pre_average) * pre_spread
    scaled = prein * pre_gain
    sums = small_total_tp(jnp.stack([jnp.sum(scaled, axis=1), jnp.sum(scaled * pre_normed, axis=1)]))
    total = (sums[0] / model_width)[:, None]
    along = (sums[1] / model_width)[:, None]
    pregain_grad = jnp.sum(prein * pre_normed, axis=0)
    prebias_grad = jnp.sum(prein, axis=0)
    input_all = low(own_columns(middle_grad, local_width) + pre_spread * (scaled - total - pre_normed * along))
    if np_:
        input_all = jnp.concatenate([input_all, jnp.zeros((np_, local_width), jnp.bfloat16)], axis=0)
    input_grad = unstripe(reorder(input_all.reshape(n_units, ROWS, local_width), rank)).astype(jnp.float32)

    small = [pregain_grad, prebias_grad, subgain_grad, subbias_grad, ffngain_grad, ffnbias_grad, midgain_grad, midbias_grad]
    joined = small_total_seq(jnp.concatenate(small))
    parts, at = [], 0
    for vector in small:
        parts.append(joined[at : at + vector.shape[0]])
        at += vector.shape[0]
    return (
        hidden_out,
        input_grad,
        parts[0],
        parts[1],
        place_two(first_pieces, second_pieces).transpose(1, 0, 2),
        parts[2],
        parts[3],
        place_pieces(*out_pieces, 1)[0],
        parts[4],
        parts[5],
        place_pieces(*up_pieces, 1)[0],
        parts[6],
        parts[7],
        place_pieces(*down_pieces, 1)[0],
    )


def shards(
    hidden_in,
    cotangent,
    valid_counts,
    pre_gain,
    pre_bias,
    qkv_weight,
    sub_gain,
    sub_bias,
    out_weight,
    ffn_gain,
    ffn_bias,
    up_weight,
    mid_gain,
    mid_bias,
    down_weight,
):
    wide = lax.axis_size("seq")
    n_units = hidden_in.shape[0] * hidden_in.shape[1] // ROWS
    span = ROWS * wide
    needed = jnp.sum((valid_counts + span - 1) // span)
    buckets = sorted({min(n, n_units) for n in BUCKETS if n < n_units} | {n_units})
    index = jnp.sum((needed > jnp.array(buckets[:-1])).astype(jnp.int32)) if len(buckets) > 1 else 0
    vectors = (pre_gain, pre_bias, sub_gain, sub_bias, ffn_gain, ffn_bias, mid_gain, mid_bias)
    weights = (qkv_weight, out_weight, up_weight, down_weight)
    operands = (hidden_in, cotangent, valid_counts, vectors, weights)
    return lax.switch(index, [functools.partial(body, n) for n in buckets], *operands)


def solution(mesh):
    placed = (
        P(None, "seq", "tp"),
        P(None, "seq", "tp"),
        P(),
        P("tp"),
        P("tp"),
        P(None, None, "tp"),
        P("tp"),
        P("tp"),
        P("tp", None),
        P("tp"),
        P("tp"),
        P(None, "tp"),
        P("tp"),
        P("tp"),
        P("tp", None),
    )
    return jax.shard_map(
        shards,
        mesh=mesh,
        in_specs=placed,
        out_specs=(
            P(None, "seq", "tp"),
            P(None, "seq", "tp"),
            P("tp"),
            P("tp"),
            P(None, None, "tp"),
            P("tp"),
            P("tp"),
            P("tp", None),
            P("tp"),
            P("tp"),
            P(None, "tp"),
            P("tp"),
            P("tp"),
            P("tp", None),
        ),
        check_vma=False,
    )
```
